512 devices in a mesh: dp: 16 (over z_hi, x, core), ctx: 32 (over z_lo, y).
Axes of the slice: x: 4, y: 8, z: 8 (z_hi: 2, z_lo: 4; z = z_hi * 4 + z_lo), core: 2. Of those that a mesh axis runs over, the one named last changes fastest.
Arguments:
- queries: bfloat16 [4096, 8192], P('ctx', 'dp'), may hold values from -150 to 150
- keys: bfloat16 [4096, 512], P('ctx'), may hold values from -6 to 6
- values: bfloat16 [4096, 512], P('ctx'), may hold values from -6 to 6
- grad_out: bfloat16 [4096, 8192], P('ctx', 'dp'), may hold values from -6 to 6
- spans: int32 [32, 2], replicated, may hold values from 0 to 63, as said below
Outputs:
- grad_queries: bfloat16 [4096, 8192], P('ctx', 'dp')
- grad_keys: bfloat16 [4096, 512], P('ctx', 'dp')
- grad_values: bfloat16 [4096, 512], P('ctx', 'dp')
The draws below stay inside these ranges and needn't reach their ends.
Inputs may be any that keep to these rules, and one draw needn't show every extreme that they name: `spans`: row r holds c and 63 - c with c < 32; every span number appears exactly once in the table.
All inputs are finite; a program needn't handle non-finite values.
Results may differ from the reference program's by a relative error of at most 0.015.
Values may be sent and summed in bfloat16 or wider, within the bound.
No kernel may reach another device: no remote copies, remote signals or barrier semaphores. Data moves between devices by JAX's collectives and lax.ppermute only.
A program may use at most 64 MiB of HBM per device.

```python
import math
import jax
import jax.numpy as jnp
from jax import lax

HD = 128
H = 64
KVH = 4
CH = 64
SPANS = 64
SEQ = 4096
GROUP = 16


def shared_keys(key):
    return jnp.clip(jax.random.normal(key, (SEQ, KVH * HD), jnp.float32), -6.0, 6.0)


def draw_keys(key, part):
    base = shared_keys(key)
    return base.astype(jnp.bfloat16)


def draw_queries(key, part):
    key = jax.random.fold_in(key, 7)
    return jnp.clip(jax.random.normal(key, (SEQ, H * HD), jnp.float32), -6.0, 6.0).astype(jnp.bfloat16)


def draw_spans(key, part):
    key = jax.random.fold_in(key, 5)
    order = jax.random.permutation(key, SPANS // 2).astype(jnp.int32)
    return jnp.stack((order, SPANS - 1 - order), axis=1).astype(jnp.int32)


def block_scale(own_key, dims, shards, least, high):
    loudness = 1.0
    for position, shards_of in shards:
        draws = jax.random.uniform(jax.random.fold_in(jax.random.fold_in(own_key, 6), position), (shards_of,), jnp.float32, least / len(shards), high / len(shards))
        loudness = loudness * jnp.repeat(jnp.exp(draws), dims[position] // shards_of).reshape((-1,) + (1,) * (len(dims) - 1 - position))
    return loudness


def gaussian(own_key, extent, width, bound, cuts=(), kind=jnp.bfloat16):
    drawn = width * jax.random.normal(own_key, extent, jnp.float32)
    if cuts:
        drawn = drawn * block_scale(own_key, extent, cuts, -0.22, 0.18)
    return jnp.clip(drawn, -bound, bound).astype(kind)


def setup_inputs(seed: int = 0) -> dict:
    streams_of = jax.random.split(jax.random.key(seed), 6)
    queries = draw_queries(jax.random.fold_in(streams_of[5], 71), 0)
    keys = draw_keys(jax.random.fold_in(streams_of[5], 71), 0)
    values = gaussian(streams_of[2], (SEQ, KVH * HD), 1.0, 6.0, ((0, 32),))
    grad_out = gaussian(streams_of[3], (SEQ, H * HD), 1.0, 6.0, ((0, 32), (1, 16)))
    spans = draw_spans(jax.random.fold_in(streams_of[5], 71), 0)
    return dict(queries=queries, keys=keys, values=values, grad_out=grad_out, spans=spans)


def reference(queries, keys, values, grad_out, spans):
    scale = 1.0 / math.sqrt(HD)
    row_ids = jnp.arange(SEQ, dtype=jnp.int32)
    pos = spans.reshape(-1)[row_ids // CH] * CH + row_ids % CH
    visible = pos[None, :] <= pos[:, None]

    def one_kv(head_kv):
        key_n = lax.dynamic_slice_in_dim(keys, (head_kv * HD).astype(jnp.int32), HD, 1)
        value_n = lax.dynamic_slice_in_dim(values, (head_kv * HD).astype(jnp.int32), HD, 1)

        def one_head(carry, member):
            acc_key, acc_value = carry
            start = ((head_kv * GROUP + member) * HD).astype(jnp.int32)
            query_h = lax.dynamic_slice_in_dim(queries, start, HD, 1)
            cotan_h = lax.dynamic_slice_in_dim(grad_out, start, HD, 1)
            scores = jnp.dot(query_h, key_n.T, preferred_element_type=jnp.float32) * scale
            top = lax.optimization_barrier(jnp.max(jnp.where(visible, scores, -1e+30), axis=-1))
            total = lax.optimization_barrier(jnp.sum(jnp.where(visible, jnp.exp(scores - top[:, None]), 0.0), axis=-1))
            lse = top + jnp.log(total)
            probs = jnp.where(visible, jnp.exp(scores - lse[:, None]), 0.0)
            probs_b = probs.astype(jnp.bfloat16)
            output = jnp.dot(probs_b, value_n, preferred_element_type=jnp.float32)
            delta = lax.optimization_barrier(jnp.sum(cotan_h.astype(jnp.float32) * output, axis=-1))
            dprob = jnp.dot(cotan_h, value_n.T, preferred_element_type=jnp.float32)
            dscore = (probs * (dprob - delta[:, None])).astype(jnp.bfloat16)
            grad_q = (jnp.dot(dscore, key_n, preferred_element_type=jnp.float32) * scale).astype(jnp.bfloat16)
            acc_key = acc_key + jnp.dot(dscore.T, query_h, preferred_element_type=jnp.float32) * scale
            acc_value = acc_value + jnp.dot(probs_b.T, cotan_h, preferred_element_type=jnp.float32)
            return ((acc_key, acc_value), grad_q)
        start_acc = (jnp.zeros((SEQ, HD), jnp.float32), jnp.zeros((SEQ, HD), jnp.float32))
        (acc_key, acc_value), grad_q = lax.scan(one_head, start_acc, jnp.arange(GROUP, dtype=jnp.int32))
        return (acc_key.astype(jnp.bfloat16), acc_value.astype(jnp.bfloat16), grad_q)
    grad_k, grad_v, grad_q = lax.map(one_kv, jnp.arange(KVH, dtype=jnp.int32))
    grad_queries = jnp.transpose(grad_q, (2, 0, 1, 3)).reshape(SEQ, H * HD)
    grad_keys = jnp.transpose(grad_k, (1, 0, 2)).reshape(SEQ, KVH * HD)
    grad_values = jnp.transpose(grad_v, (1, 0, 2)).reshape(SEQ, KVH * HD)
    return (grad_queries, grad_keys, grad_values)
```

```python
import functools
import math

import jax
import jax.numpy as jnp
from jax import lax
from jax.experimental import pallas as pl
from jax.experimental.pallas import tpu as pltpu
from jax.sharding import Mesh
from jax.sharding import PartitionSpec as P

HD = 128
H = 64
KVH = 4
SPAN = 64
SUB = 16
TILE = 256
LOW = -1e30
FLOOR = -1e29
SCALE = 1.0 / math.sqrt(HD)
EXP2 = SCALE * math.log2(math.e)
VM = pltpu.VMEM
F32 = jnp.float32
BF16 = jnp.bfloat16
NT = (((1,), (1,)), ((), ()))
NN = (((1,), (0,)), ((), ()))


def dot(a, b, dims=NN):
    return lax.dot_general(a, b, dims, preferred_element_type=F32)


def pick_kernel(meta, keys, values, kv_out, held, sems):
    col = pl.multiple_of(meta[0] * HD, HD)
    copies = []
    for which, ref in enumerate((keys, values)):
        for half in range(2):
            at = which * 2 + half
            row = pl.multiple_of(half * SPAN + meta[1] * SUB, SUB)
            copies.append(
                pltpu.make_async_copy(
                    ref.at[pl.ds(row, SUB), pl.ds(col, HD)], held.at[at * SUB : (at + 1) * SUB, :], sems.at[at]
                )
            )
    for copy in copies:
        copy.start()
    for copy in copies:
        copy.wait()
    for dest in range(kv_out.shape[0]):
        kv_out[dest] = held[...]


def pair_kernel(queries, cotan, out):
    out[0] = queries[...]
    out[1] = cotan[...]


def load(meta, spans, kv, own, other, ks, vs, qs, gs):
    for src in range(kv.shape[0]):
        for half in range(2):
            at = pl.multiple_of(spans[src, half] * SUB, SUB)
            ks[pl.ds(at, SUB), :] = kv[src, half * SUB : (half + 1) * SUB, :]
            vs[pl.ds(at, SUB), :] = kv[src, (2 + half) * SUB : (3 + half) * SUB, :]
    heads = own.shape[3] // HD
    for pair, ref in enumerate((own, other)):
        for core in range(2):
            for head in range(heads):
                at = (((pair ^ meta[4]) * 2 + core) * heads + head) * SPAN
                at = pl.multiple_of(at, SPAN)
                for half in range(2):
                    rows = slice(half * SPAN, (half + 1) * SPAN)
                    cols = slice(head * HD, (head + 1) * HD)
                    rank = half ^ meta[5]
                    qs[rank, pl.ds(at, SPAN), :] = ref[core, 0, rows, cols]
                    gs[rank, pl.ds(at, SPAN), :] = ref[core, 1, rows, cols]


def offsets(width):
    key = lax.broadcasted_iota(jnp.int32, (TILE, width), 0)
    row = lax.broadcasted_iota(jnp.int32, (TILE, width), 1)
    return (key // SUB) * SPAN + key % SUB - row % SPAN


def units(meta):
    early = meta[2] < 16
    return (
        (0, 0, True),
        (1, 0, False),
        (1, 1, False),
        (1, 2, True),
        (jnp.where(early, 1, 0), jnp.where(early, 3, 1), True),
    )


def bound(meta, half, tile):
    span = jnp.where(half == 0, meta[2], meta[3])
    return span * SPAN - tile * (TILE // SUB * SPAN) - meta[1] * SUB


WIDTH = 256


def stats_kernel(meta, spans, kv, own, other, out, ks, vs, qs, gs, part):
    load(meta, spans, kv, own, other, ks, vs, qs, gs)
    rows = qs.shape[1]
    for unit, (half, tile, masked) in enumerate(units(meta)):
        at = pl.multiple_of(tile * TILE, TILE) if unit == 4 else tile * TILE
        key = ks[pl.ds(at, TILE), :]
        value = vs[pl.ds(at, TILE), :]
        for first in range(0, rows, WIDTH):
            cols = slice(first, first + WIDTH)
            score = dot(key, qs[half, cols, :], NT)
            if masked:
                score = jnp.where(offsets(WIDTH) <= bound(meta, half, tile), score, LOW)
            top = jnp.maximum(jnp.max(score, axis=0, keepdims=True), FLOOR)
            weight = jnp.exp2((score - top) * EXP2)
            dprob = dot(value, gs[half, cols, :], NT)
            part[unit, 0:1, cols] = top
            part[unit, 1:2, cols] = jnp.sum(weight, axis=0, keepdims=True)
            part[unit, 2:3, cols] = jnp.sum(weight * dprob, axis=0, keepdims=True)
    early = meta[2] < 16
    for half, mine in enumerate(((0,), (1, 2, 3))):
        extra = jnp.where(early, F32(half), F32(1 - half)) > 0.5
        tops = [part[unit, 0:1, :] for unit in mine] + [jnp.where(extra, part[4, 0:1, :], FLOOR)]
        top = functools.reduce(jnp.maximum, tops)
        total = jnp.zeros_like(top)
        weighted = jnp.zeros_like(top)
        for unit, unit_top in zip(mine + (4,), tops):
            factor = jnp.exp2((unit_top - top) * EXP2)
            if unit == 4:
                factor = jnp.where(extra, factor, 0.0)
            total = total + factor * part[unit, 1:2, :]
            weighted = weighted + factor * part[unit, 2:3, :]
        out[half * 3 : half * 3 + 1, :] = top
        out[half * 3 + 1 : half * 3 + 2, :] = total
        out[half * 3 + 2 : half * 3 + 3, :] = weighted
    out[6:8, :] = jnp.zeros((2, rows), F32)


def sort_keys(spans, kv, first, out):
    for src in range(kv.shape[0]):
        for half in range(2):
            at = pl.multiple_of(spans[src, half] * SUB, SUB)
            out[pl.ds(at, SUB), :] = kv[src, (first + half) * SUB : (first + half + 1) * SUB, :]


def key_grads_kernel(
    meta, spans, stats, kv, own, other, dkv_out, dscore_out,
    ks, vs, qs, gs, row_stats, probs_b, dk, dv,
):
    load(meta, spans, kv, own, other, ks, vs, qs, gs)
    rows = qs.shape[1]
    for half in range(2):
        tops = [stats[src, half * 3 : half * 3 + 1, :] for src in range(4)]
        top = functools.reduce(jnp.maximum, tops)
        factors = [jnp.exp2((one - top) * EXP2) for one in tops]
        total = sum(factors[src] * stats[src, half * 3 + 1 : half * 3 + 2, :] for src in range(4))
        weighted = sum(factors[src] * stats[src, half * 3 + 2 : half * 3 + 3, :] for src in range(4))
        row_stats[half, 0:1, :] = top
        row_stats[half, 1:2, :] = 1.0 / total
        row_stats[half, 2:3, :] = weighted / total
    dk[3 * TILE :, :] = jnp.zeros((TILE, HD), F32)
    dv[3 * TILE :, :] = jnp.zeros((TILE, HD), F32)
    for unit, (half, tile, masked) in enumerate(units(meta)):
        at = pl.multiple_of(tile * TILE, TILE) if unit == 4 else tile * TILE
        key = ks[pl.ds(at, TILE), :]
        value = vs[pl.ds(at, TILE), :]
        for first in range(0, rows, WIDTH):
            cols = slice(first, first + WIDTH)
            score = dot(key, qs[half, cols, :], NT)
            if masked:
                score = jnp.where(offsets(WIDTH) <= bound(meta, half, tile), score, LOW)
            prob = jnp.exp2((score - row_stats[half, 0:1, cols]) * EXP2) * row_stats[half, 1:2, cols]
            dprob = dot(value, gs[half, cols, :], NT)
            dscore = prob * (dprob - row_stats[half, 2:3, cols])
            probs_b[unit % 2, :, cols] = prob.astype(BF16)
            dscore_out[unit, :, cols] = dscore.astype(BF16)
        dv_tile = dot(probs_b[unit % 2], gs[half])
        dk_tile = dot(dscore_out[unit], qs[half])
        keys_of = pl.ds(at, TILE)
        if unit in (0, 2, 3):
            dv[keys_of, :] = dv_tile
            dk[keys_of, :] = dk_tile
        else:
            dv[keys_of, :] += dv_tile
            dk[keys_of, :] += dk_tile
    for dest in range(dkv_out.shape[0]):
        for half in range(2):
            at = pl.multiple_of(spans[dest, half] * SUB, SUB)
            dkv_out[dest, half * SUB : (half + 1) * SUB, :] = (dk[pl.ds(at, SUB), :] * SCALE).astype(BF16)
            dkv_out[dest, (2 + half) * SUB : (3 + half) * SUB, :] = dv[pl.ds(at, SUB), :].astype(BF16)


def query_grads_kernel(meta, spans, kv, dscore, out_0, out_1, out_2, out_3, ks, kt, dq, back):
    sort_keys(spans, kv, 0, ks)
    kt[...] = ks[...].T
    for unit, (half, tile, _) in enumerate(units(meta)):
        at = pl.multiple_of(tile * TILE, TILE) if unit == 4 else tile * TILE
        dq_half = dot(kt[:, pl.ds(at, TILE)], dscore[unit])
        if unit in (0, 1):
            dq[half] = dq_half
        else:
            dq[half] += dq_half
    heads = out_0.shape[1] // HD
    for half in range(2):
        back[...] = (dq[half ^ meta[5]] * SCALE).T.astype(BF16)
        for step, out in enumerate((out_0, out_1, out_2, out_3)):
            for head in range(heads):
                at = pl.multiple_of(((meta[1] ^ step) * heads + head) * SPAN, SPAN)
                out[half * SPAN : (half + 1) * SPAN, head * HD : (head + 1) * HD] = back[pl.ds(at, SPAN), :]


def split_kernel(whole, sharer, grad_keys, grad_values):
    wide = grad_keys.shape[1]
    for which, out in enumerate((grad_keys, grad_values)):
        for half in range(2):
            for src in range(4):
                at = (which * 2 + half) * SUB
                block = whole[src, at : at + SUB, :]
                part = block[:, 3 * wide :]
                for mine in range(3):
                    part = jnp.where(sharer[0] == mine, block[:, mine * wide : (mine + 1) * wide], part)
                row = half * SPAN + src * SUB
                out[row : row + SUB, :] = part


def call(kernel, out_shape, scratch, flops, spaces, *args, limit=32):
    return pl.pallas_call(
        kernel,
        out_shape=out_shape,
        in_specs=[pl.BlockSpec(memory_space={"s": pltpu.SMEM, "v": VM, "a": pl.ANY}[space]) for space in spaces],
        out_specs=jax.tree.map(lambda _: pl.BlockSpec(memory_space=VM), out_shape),
        scratch_shapes=scratch,
        cost_estimate=pl.CostEstimate(flops=flops, bytes_accessed=1 << 20, transcendentals=0),
        compiler_params=pltpu.CompilerParams(vmem_limit_bytes=limit << 20),
    )(*args)


def on_device(queries, keys, values, grad_out, spans):
    rows, width = queries.shape
    ctx_count = lax.axis_size("ctx")
    group_index = lax.axis_index("group")
    x_index = lax.axis_index("pair")
    sharer = x_index * 2 + lax.axis_index("core")
    ctx_index = lax.axis_index("ctx")
    mine = lax.dynamic_slice_in_dim(spans, ctx_index, 1, 0).reshape(2)
    low, high = jnp.minimum(mine[0], mine[1]), jnp.maximum(mine[0], mine[1])
    meta = jnp.stack((group_index, sharer, low, high, x_index, mine[0] > mine[1])).astype(jnp.int32)
    pick_meta = jnp.stack((group_index, sharer)).astype(jnp.int32)
    sds = jax.ShapeDtypeStruct
    blocks = sds((ctx_count, 4 * SUB, HD), BF16)
    kv_send = call(
        pick_kernel,
        blocks,
        [VM((4 * SUB, HD), BF16), pltpu.SemaphoreType.DMA((4,))],
        1 << 20,
        "saa",
        pick_meta, keys, values,
        limit=60,
    )
    kv = lax.all_to_all(kv_send, "ctx", 0, 0, tiled=True)
    qd = call(pair_kernel, sds((2, rows, width), BF16), [], 1 << 20, "vv", queries, grad_out)
    crossed = lax.ppermute(qd, "pair", [(0, 1), (1, 0)])
    own = lax.all_gather(qd, "core", axis=0)
    other = lax.all_gather(crossed, "core", axis=0)
    stacked = 2 * 2 * (width // HD) * SPAN
    keys_held = 2 * ctx_count * SUB
    common = [VM((keys_held, HD), BF16)] * 2 + [VM((2, stacked, HD), BF16)] * 2
    stats = call(
        stats_kernel,
        sds((8, stacked), F32),
        common + [VM((5, 8, stacked), F32)],
        1 << 30,
        "ssvvv",
        meta, spans, kv, own, other,
    )
    stats_all = lax.all_gather(stats, ("pair", "core"), axis=0)
    dkv_send, dscore = call(
        key_grads_kernel,
        (blocks, sds((5, TILE, stacked), BF16)),
        common
        + [
            VM((2, 8, stacked), F32),
            VM((2, TILE, stacked), BF16),
            VM((keys_held, HD), F32),
            VM((keys_held, HD), F32),
        ],
        1 << 31,
        "ssvvvv",
        meta, spans, stats_all, kv, own, other,
    )
    dkv = lax.all_to_all(dkv_send, "ctx", 0, 0, tiled=True)
    dq_mine, *dq_send = call(
        query_grads_kernel,
        (sds((rows, width), BF16),) * 4,
        [
            VM((keys_held, HD), BF16),
            VM((HD, keys_held), BF16),
            VM((2, HD, stacked), F32),
            VM((stacked, HD), BF16),
        ],
        1 << 31,
        "ssvv",
        meta, spans, kv, dscore,
    )
    grad_queries = dq_mine.astype(F32)
    for step, piece in enumerate(dq_send, 1):
        grad_queries += lax.ppermute(piece, ("pair", "core"), [(i, i ^ step) for i in range(4)]).astype(F32)
    grad_queries = grad_queries.astype(BF16)
    summed = jnp.sum(dkv.astype(F32), axis=0).astype(BF16)
    whole = lax.all_gather(summed, ("pair", "core"), axis=0)
    part = sds((rows, HD // 4), BF16)
    grad_keys, grad_values = call(split_kernel, (part, part), [], 1 << 20, "vs", whole, sharer.reshape(1), limit=60)
    return (grad_queries, grad_keys, grad_values)


def solution(mesh):
    dp, ctx = mesh.devices.shape
    fine = Mesh(mesh.devices.reshape(dp // 4, 2, 2, ctx), ("group", "pair", "core", "ctx"))
    heads = ("group", "pair", "core")
    return jax.shard_map(
        on_device,
        mesh=fine,
        in_specs=(P("ctx", heads), P("ctx", None), P("ctx", None), P("ctx", heads), P()),
        out_specs=(P("ctx", heads), P("ctx", heads), P("ctx", heads)),
        check_vma=False,
    )
```

```python
import functools
import math

import jax
import jax.numpy as jnp
from jax import lax
from jax.experimental import pallas as pl
from jax.experimental.pallas import tpu as pltpu
from jax.sharding import Mesh
from jax.sharding import PartitionSpec as P

HD = 128
H = 64
KVH = 4
SPAN = 64
SUB = 16
TILE = 256
LOW = -1e30
FLOOR = -1e29
SCALE = 1.0 / math.sqrt(HD)
EXP2 = SCALE * math.log2(math.e)
VM = pltpu.VMEM
F32 = jnp.float32
BF16 = jnp.bfloat16
NT = (((1,), (1,)), ((), ()))
NN = (((1,), (0,)), ((), ()))


def dot(a, b, dims=NN):
    return lax.dot_general(a, b, dims, preferred_element_type=F32)


def place(spans=None):
    pair = lax.axis_index("pair")
    sharer = pair * 2 + lax.axis_index("core")
    if spans is None:
        return lax.axis_index("group"), sharer
    ctx = lax.axis_index("ctx")
    first, second = spans[0, ctx], spans[1, ctx]
    swapped = jnp.where(first > second, 1, 0)
    return lax.axis_index("group"), sharer, jnp.minimum(first, second), jnp.maximum(first, second), pair, swapped


def pick_kernel(keys, values, kv_out, held, sems):
    meta = place()
    col = pl.multiple_of(meta[0] * HD, HD)
    copies = []
    for which, ref in enumerate((keys, values)):
        for half in range(2):
            at = which * 2 + half
            row = pl.multiple_of(half * SPAN + meta[1] * SUB, SUB)
            copies.append(
                pltpu.make_async_copy(
                    ref.at[pl.ds(row, SUB), pl.ds(col, HD)], held.at[at * SUB : (at + 1) * SUB, :], sems.at[at]
                )
            )
    for copy in copies:
        copy.start()
    for copy in copies:
        copy.wait()
    for dest in range(kv_out.shape[0]):
        kv_out[dest] = held[...]


def pair_kernel(queries, cotan, out):
    out[0] = queries[...]
    out[1] = cotan[...]


def load(meta, spans, kv, own, other, ks, vs, qs, gs):
    for src in range(kv.shape[0]):
        for half in range(2):
            at = pl.multiple_of(spans[half, src] * SUB, SUB)
            ks[pl.ds(at, SUB), :] = kv[src, half * SUB : (half + 1) * SUB, :]
            vs[pl.ds(at, SUB), :] = kv[src, (2 + half) * SUB : (3 + half) * SUB, :]
    heads = own.shape[3] // HD
    for pair, ref in enumerate((own, other)):
        for core in range(2):
            for head in range(heads):
                at = (((pair ^ meta[4]) * 2 + core) * heads + head) * SPAN
                at = pl.multiple_of(at, SPAN)
                for half in range(2):
                    rows = slice(half * SPAN, (half + 1) * SPAN)
                    cols = slice(head * HD, (head + 1) * HD)
                    rank = half ^ meta[5]
                    qs[rank, pl.ds(at, SPAN), :] = ref[core, 0, rows, cols]
                    gs[rank, pl.ds(at, SPAN), :] = ref[core, 1, rows, cols]


def offsets():
    key = lax.broadcasted_iota(jnp.int32, (TILE, WIDTH), 0)
    row = lax.broadcasted_iota(jnp.int32, (TILE, WIDTH), 1)
    return (key >> 4) * SPAN + (key & (SUB - 1)) - (row & (SPAN - 1))


def units(meta):
    early = meta[2] < 16
    return (
        (0, 0, True),
        (1, 0, False),
        (1, 1, False),
        (1, 2, True),
        (jnp.where(early, 1, 0), jnp.where(early, 3, 1), True),
    )


def bound(meta, half, tile):
    span = jnp.where(half == 0, meta[2], meta[3])
    return span * SPAN - tile * (TILE // SUB * SPAN) - meta[1] * SUB


WIDTH = 256


def stats_kernel(spans, kv, own, other, out, ks, vs, qs, gs, part, off):
    meta = place(spans)
    off[...] = offsets()
    load(meta, spans, kv, own, other, ks, vs, qs, gs)
    rows = qs.shape[1]
    for unit, (half, tile, masked) in enumerate(units(meta)):
        at = pl.multiple_of(tile * TILE, TILE) if unit == 4 else tile * TILE
        key = ks[pl.ds(at, TILE), :]
        value = vs[pl.ds(at, TILE), :]
        for first in range(0, rows, WIDTH):
            cols = slice(first, first + WIDTH)
            score = dot(key, qs[half, cols, :], NT)
            if masked:
                score = jnp.where(off[...] <= bound(meta, half, tile), score, LOW)
            top = jnp.maximum(jnp.max(score, axis=0, keepdims=True), FLOOR)
            weight = jnp.exp2((score - top) * EXP2)
            dprob = dot(value, gs[half, cols, :], NT)
            part[unit, 0:1, cols] = top
            part[unit, 1:2, cols] = jnp.sum(weight, axis=0, keepdims=True)
            part[unit, 2:3, cols] = jnp.sum(weight * dprob, axis=0, keepdims=True)
    early = meta[2] < 16
    for half, mine in enumerate(((0,), (1, 2, 3))):
        extra = jnp.where(early, F32(half), F32(1 - half)) > 0.5
        tops = [part[unit, 0:1, :] for unit in mine] + [jnp.where(extra, part[4, 0:1, :], FLOOR)]
        top = functools.reduce(jnp.maximum, tops)
        total = jnp.zeros_like(top)
        weighted = jnp.zeros_like(top)
        for unit, unit_top in zip(mine + (4,), tops):
            factor = jnp.exp2((unit_top - top) * EXP2)
            if unit == 4:
                factor = jnp.where(extra, factor, 0.0)
            total = total + factor * part[unit, 1:2, :]
            weighted = weighted + factor * part[unit, 2:3, :]
        out[half * 3 : half * 3 + 1, :] = top
        out[half * 3 + 1 : half * 3 + 2, :] = total
        out[half * 3 + 2 : half * 3 + 3, :] = weighted
    out[6:8, :] = jnp.zeros((2, rows), F32)


def grads_kernel(
    spans, stats, kv, own, other, dkv_out, dq_0, dq_1, dq_2, dq_3,
    ks, vs, qs, gs, row_stats, probs_b, dscore_b, dk, dv, dq, kt, back, off,
):
    meta = place(spans)
    off[...] = offsets()
    load(meta, spans, kv, own, other, ks, vs, qs, gs)
    kt[...] = ks[...].T
    rows = qs.shape[1]
    for half in range(2):
        tops = [stats[src, half * 3 : half * 3 + 1, :] for src in range(4)]
        top = functools.reduce(jnp.maximum, tops)
        factors = [jnp.exp2((one - top) * EXP2) for one in tops]
        total = sum(factors[src] * stats[src, half * 3 + 1 : half * 3 + 2, :] for src in range(4))
        weighted = sum(factors[src] * stats[src, half * 3 + 2 : half * 3 + 3, :] for src in range(4))
        row_stats[half, 0:1, :] = top
        row_stats[half, 1:2, :] = 1.0 / total
        row_stats[half, 2:3, :] = weighted / total
    dk[3 * TILE :, :] = jnp.zeros((TILE, HD), F32)
    dv[3 * TILE :, :] = jnp.zeros((TILE, HD), F32)
    for unit, (half, tile, masked) in enumerate(units(meta)):
        at = pl.multiple_of(tile * TILE, TILE) if unit == 4 else tile * TILE
        key = ks[pl.ds(at, TILE), :]
        value = vs[pl.ds(at, TILE), :]
        for first in range(0, rows, WIDTH):
            cols = slice(first, first + WIDTH)
            score = dot(key, qs[half, cols, :], NT)
            if masked:
                score = jnp.where(off[...] <= bound(meta, half, tile), score, LOW)
            prob = jnp.exp2((score - row_stats[half, 0:1, cols]) * EXP2) * row_stats[half, 1:2, cols]
            dprob = dot(value, gs[half, cols, :], NT)
            dscore = prob * (dprob - row_stats[half, 2:3, cols])
            probs_b[unit % 2, :, cols] = prob.astype(BF16)
            dscore_b[unit % 2, :, cols] = dscore.astype(BF16)
        dv_tile = dot(probs_b[unit % 2], gs[half])
        dk_tile = dot(dscore_b[unit % 2], qs[half])
        dq_half = dot(kt[:, pl.ds(at, TILE)], dscore_b[unit % 2])
        keys_of = pl.ds(at, TILE)
        if unit in (0, 2, 3):
            dv[keys_of, :] = dv_tile
            dk[keys_of, :] = dk_tile
        else:
            dv[keys_of, :] += dv_tile
            dk[keys_of, :] += dk_tile
        if unit in (0, 1):
            dq[half] = dq_half
        else:
            dq[half] += dq_half
    for dest in range(dkv_out.shape[0]):
        for half in range(2):
            at = pl.multiple_of(spans[half, dest] * SUB, SUB)
            dkv_out[dest, half * SUB : (half + 1) * SUB, :] = (dk[pl.ds(at, SUB), :] * SCALE).astype(BF16)
            dkv_out[dest, (2 + half) * SUB : (3 + half) * SUB, :] = dv[pl.ds(at, SUB), :].astype(BF16)
    heads = dq_0.shape[1] // HD
    for half in range(2):
        back[...] = (dq[half ^ meta[5]] * SCALE).T.astype(BF16)
        for step, out in enumerate((dq_0, dq_1, dq_2, dq_3)):
            for head in range(heads):
                at = pl.multiple_of(((meta[1] ^ step) * heads + head) * SPAN, SPAN)
                out[half * SPAN : (half + 1) * SPAN, head * HD : (head + 1) * HD] = back[pl.ds(at, SPAN), :]


def split_kernel(whole, grad_keys, grad_values, turned):
    _, sharer = place()
    wide = grad_keys.shape[0]
    for which, out in enumerate((grad_keys, grad_values)):
        pieces = []
        for half in range(2):
            at = (which * 2 + half) * SUB
            pieces += [whole[src, at : at + SUB, :] for src in range(4)]
        turned[...] = jnp.concatenate(pieces, axis=0).astype(F32).T
        out[...] = turned[pl.ds(pl.multiple_of(sharer * wide, wide), wide), :].astype(BF16)


def call(kernel, out_shape, scratch, flops, spaces, *args, limit=32, outs=None):
    return pl.pallas_call(
        kernel,
        out_shape=out_shape,
        in_specs=[pl.BlockSpec(memory_space={"s": pltpu.SMEM, "v": VM, "a": pl.ANY}[space]) for space in spaces],
        out_specs=outs or jax.tree.map(lambda _: pl.BlockSpec(memory_space=VM), out_shape),
        scratch_shapes=scratch,
        cost_estimate=pl.CostEstimate(flops=flops, bytes_accessed=1 << 20, transcendentals=0),
        compiler_params=pltpu.CompilerParams(vmem_limit_bytes=limit << 20),
    )(*args)


def on_device(queries, keys, values, grad_out, spans):
    rows, width = queries.shape
    ctx_count = lax.axis_size("ctx")
    spans = spans.T
    sds = jax.ShapeDtypeStruct
    blocks = sds((ctx_count, 4 * SUB, HD), BF16)
    kv_send = call(
        pick_kernel,
        blocks,
        [VM((4 * SUB, HD), BF16), pltpu.SemaphoreType.DMA((4,))],
        1 << 20,
        "aa",
        keys, values,
        limit=60,
    )
    kv = lax.all_to_all(kv_send, "ctx", 0, 0, tiled=True)
    qd = call(pair_kernel, sds((2, rows, width), BF16), [], 1 << 20, "vv", queries, grad_out)
    crossed = lax.ppermute(qd, "pair", [(0, 1), (1, 0)])
    own = lax.all_gather(qd, "core", axis=0)
    other = lax.all_gather(crossed, "core", axis=0)
    stacked = 2 * 2 * (width // HD) * SPAN
    keys_held = 2 * ctx_count * SUB
    common = [VM((keys_held, HD), BF16)] * 2 + [VM((2, stacked, HD), BF16)] * 2
    mask = VM((TILE, WIDTH), jnp.int32)
    stats = call(
        stats_kernel,
        sds((8, stacked), F32),
        common + [VM((5, 8, stacked), F32), mask],
        1 << 30,
        "svvv",
        spans, kv, own, other,
    )
    stats_all = lax.all_gather(stats, ("pair", "core"), axis=0)
    dkv_send, dq_mine, *dq_send = call(
        grads_kernel,
        (blocks,) + (sds((rows, width), BF16),) * 4,
        common
        + [
            VM((2, 8, stacked), F32),
            VM((2, TILE, stacked), BF16),
            VM((2, TILE, stacked), BF16),
            VM((keys_held, HD), F32),
            VM((keys_held, HD), F32),
            VM((2, HD, stacked), F32),
            VM((HD, keys_held), BF16),
            VM((stacked, HD), BF16),
            mask,
        ],
        1 << 31,
        "svvvv",
        spans, stats_all, kv, own, other,
    )
    dkv = lax.all_to_all(dkv_send, "ctx", 0, 0, tiled=True)
    grad_queries = dq_mine.astype(F32)
    for step, piece in enumerate(dq_send, 1):
        grad_queries += lax.ppermute(piece, ("pair", "core"), [(i, i ^ step) for i in range(4)]).astype(F32)
    grad_queries = grad_queries.astype(BF16)
    summed = jnp.sum(dkv.astype(F32), axis=0).astype(BF16)
    whole = lax.all_gather(summed, ("pair", "core"), axis=0)
    part = sds((HD // 4, rows), BF16)
    grad_keys, grad_values = call(split_kernel, (part, part), [VM((HD, rows), F32)], 1 << 20, "v", whole, limit=60)
    return (grad_queries, grad_keys.T, grad_values.T)


def solution(mesh):
    dp, ctx = mesh.devices.shape
    fine = Mesh(mesh.devices.reshape(dp // 4, 2, 2, ctx), ("group", "pair", "core", "ctx"))
    heads = ("group", "pair", "core")
    return jax.shard_map(
        on_device,
        mesh=fine,
        in_specs=(P("ctx", heads), P("ctx", None), P("ctx", None), P("ctx", heads), P()),
        out_specs=(P("ctx", heads), P("ctx", heads), P("ctx", heads)),
        check_vma=False,
    )
```

```python
import functools
import math

import jax
import jax.numpy as jnp
from jax import lax
from jax.experimental import pallas as pl
from jax.experimental.pallas import tpu as pltpu
from jax.sharding import Mesh
from jax.sharding import PartitionSpec as P

HD = 128
H = 64
KVH = 4
SPAN = 64
SUB = 16
TILE = 256
LOW = -1e30
FLOOR = -1e29
SCALE = 1.0 / math.sqrt(HD)
EXP2 = SCALE * math.log2(math.e)
VM = pltpu.VMEM
F32 = jnp.float32
BF16 = jnp.bfloat16
NT = (((1,), (1,)), ((), ()))
NN = (((1,), (0,)), ((), ()))


def dot(a, b, dims=NN):
    return lax.dot_general(a, b, dims, preferred_element_type=F32)


def place(spans=None):
    pair = lax.axis_index("pair")
    sharer = pair * 2 + lax.axis_index("core")
    if spans is None:
        return lax.axis_index("group"), sharer
    ctx = lax.axis_index("ctx")
    first, second = spans[0, ctx], spans[1, ctx]
    swapped = jnp.where(first > second, 1, 0)
    return lax.axis_index("group"), sharer, jnp.minimum(first, second), jnp.maximum(first, second), pair, swapped


def pick_kernel(keys, values, kv_out, held, sems):
    meta = place()
    col = pl.multiple_of(meta[0] * HD, HD)
    copies = []
    for which, ref in enumerate((keys, values)):
        for half in range(2):
            at = which * 2 + half
            row = pl.multiple_of(half * SPAN + meta[1] * SUB, SUB)
            copies.append(
                pltpu.make_async_copy(
                    ref.at[pl.ds(row, SUB), pl.ds(col, HD)], held.at[at * SUB : (at + 1) * SUB, :], sems.at[at]
                )
            )
    for copy in copies:
        copy.start()
    for copy in copies:
        copy.wait()
    for dest in range(kv_out.shape[0]):
        kv_out[dest] = held[...]


def pair_kernel(queries, cotan, spans, out, spans_out):
    spans_out[...] = spans[...]
    out[0] = queries[...]
    out[1] = cotan[...]


def load(meta, spans, kv, own, other, ks, vs, qs, gs):
    for src in range(kv.shape[0]):
        for half in range(2):
            at = pl.multiple_of(spans[half, src] * SUB, SUB)
            ks[pl.ds(at, SUB), :] = kv[src, half * SUB : (half + 1) * SUB, :]
            vs[pl.ds(at, SUB), :] = kv[src, (2 + half) * SUB : (3 + half) * SUB, :]
    heads = own.shape[3] // HD
    for pair, ref in enumerate((own, other)):
        for core in range(2):
            for head in range(heads):
                at = (((pair ^ meta[4]) * 2 + core) * heads + head) * SPAN
                at = pl.multiple_of(at, SPAN)
                for half in range(2):
                    rows = slice(half * SPAN, (half + 1) * SPAN)
                    cols = slice(head * HD, (head + 1) * HD)
                    rank = half ^ meta[5]
                    qs[rank, pl.ds(at, SPAN), :] = ref[core, 0, rows, cols]
                    gs[rank, pl.ds(at, SPAN), :] = ref[core, 1, rows, cols]


def offsets():
    key = lax.broadcasted_iota(jnp.int32, (TILE, WIDTH), 0)
    row = lax.broadcasted_iota(jnp.int32, (TILE, WIDTH), 1)
    return (key >> 4) * SPAN + (key & (SUB - 1)) - (row & (SPAN - 1))


def units(meta):
    early = meta[2] < 16
    return (
        (0, 0, True),
        (1, 0, False),
        (1, 1, False),
        (1, 2, True),
        (jnp.where(early, 1, 0), jnp.where(early, 3, 1), True),
    )


def bound(meta, half, tile):
    span = jnp.where(half == 0, meta[2], meta[3])
    return span * SPAN - tile * (TILE // SUB * SPAN) - meta[1] * SUB


WIDTH = 256


def stats_kernel(spans, kv, own, other, out, ks, vs, qs, gs, part, off):
    meta = place(spans)
    off[...] = offsets()
    load(meta, spans, kv, own, other, ks, vs, qs, gs)
    rows = qs.shape[1]
    for unit, (half, tile, masked) in enumerate(units(meta)):
        at = pl.multiple_of(tile * TILE, TILE) if unit == 4 else tile * TILE
        key = ks[pl.ds(at, TILE), :]
        value = vs[pl.ds(at, TILE), :]
        for first in range(0, rows, WIDTH):
            cols = slice(first, first + WIDTH)
            score = dot(key, qs[half, cols, :], NT)
            if masked:
                score = jnp.where(off[...] <= bound(meta, half, tile), score, LOW)
            top = jnp.maximum(jnp.max(score, axis=0, keepdims=True), FLOOR)
            weight = jnp.exp2((score - top) * EXP2)
            dprob = dot(value, gs[half, cols, :], NT)
            part[unit, 0:1, cols] = top
            part[unit, 1:2, cols] = jnp.sum(weight, axis=0, keepdims=True)
            part[unit, 2:3, cols] = jnp.sum(weight * dprob, axis=0, keepdims=True)
    early = meta[2] < 16
    for half, mine in enumerate(((0,), (1, 2, 3))):
        extra = jnp.where(early, F32(half), F32(1 - half)) > 0.5
        tops = [part[unit, 0:1, :] for unit in mine] + [jnp.where(extra, part[4, 0:1, :], FLOOR)]
        top = functools.reduce(jnp.maximum, tops)
        total = jnp.zeros_like(top)
        weighted = jnp.zeros_like(top)
        for unit, unit_top in zip(mine + (4,), tops):
            factor = jnp.exp2((unit_top - top) * EXP2)
            if unit == 4:
                factor = jnp.where(extra, factor, 0.0)
            total = total + factor * part[unit, 1:2, :]
            weighted = weighted + factor * part[unit, 2:3, :]
        out[half * 3 : half * 3 + 1, :] = top
        out[half * 3 + 1 : half * 3 + 2, :] = total
        out[half * 3 + 2 : half * 3 + 3, :] = weighted
    out[6:8, :] = jnp.zeros((2, rows), F32)


def grads_kernel(
    spans, stats, kv, own, other, dkv_out, dq_0, dq_1, dq_2, dq_3,
    ks, vs, qs, gs, row_stats, probs_b, dscore_b, dk, dv, dq, kt, back, off,
):
    meta = place(spans)
    off[...] = offsets()
    load(meta, spans, kv, own, other, ks, vs, qs, gs)
    kt[...] = ks[...].T
    rows = qs.shape[1]
    for half in range(2):
        tops = [stats[src, half * 3 : half * 3 + 1, :] for src in range(4)]
        top = functools.reduce(jnp.maximum, tops)
        factors = [jnp.exp2((one - top) * EXP2) for one in tops]
        total = sum(factors[src] * stats[src, half * 3 + 1 : half * 3 + 2, :] for src in range(4))
        weighted = sum(factors[src] * stats[src, half * 3 + 2 : half * 3 + 3, :] for src in range(4))
        row_stats[half, 0:1, :] = top
        row_stats[half, 1:2, :] = 1.0 / total
        row_stats[half, 2:3, :] = weighted / total
    dk[3 * TILE :, :] = jnp.zeros((TILE, HD), F32)
    dv[3 * TILE :, :] = jnp.zeros((TILE, HD), F32)
    for unit, (half, tile, masked) in enumerate(units(meta)):
        at = pl.multiple_of(tile * TILE, TILE) if unit == 4 else tile * TILE
        key = ks[pl.ds(at, TILE), :]
        value = vs[pl.ds(at, TILE), :]
        for first in range(0, rows, WIDTH):
            cols = slice(first, first + WIDTH)
            score = dot(key, qs[half, cols, :], NT)
            if masked:
                score = jnp.where(off[...] <= bound(meta, half, tile), score, LOW)
            prob = jnp.exp2((score - row_stats[half, 0:1, cols]) * EXP2) * row_stats[half, 1:2, cols]
            dprob = dot(value, gs[half, cols, :], NT)
            dscore = prob * (dprob - row_stats[half, 2:3, cols])
            probs_b[unit % 2, :, cols] = prob.astype(BF16)
            dscore_b[unit % 2, :, cols] = dscore.astype(BF16)
        dv_tile = dot(probs_b[unit % 2], gs[half])
        dk_tile = dot(dscore_b[unit % 2], qs[half])
        dq_half = dot(kt[:, pl.ds(at, TILE)], dscore_b[unit % 2])
        keys_of = pl.ds(at, TILE)
        if unit in (0, 2, 3):
            dv[keys_of, :] = dv_tile
            dk[keys_of, :] = dk_tile
        else:
            dv[keys_of, :] += dv_tile
            dk[keys_of, :] += dk_tile
        if unit in (0, 1):
            dq[half] = dq_half
        else:
            dq[half] += dq_half
    for dest in range(dkv_out.shape[0]):
        for half in range(2):
            at = pl.multiple_of(spans[half, dest] * SUB, SUB)
            dkv_out[dest, half * SUB : (half + 1) * SUB, :] = (dk[pl.ds(at, SUB), :] * SCALE).astype(BF16)
            dkv_out[dest, (2 + half) * SUB : (3 + half) * SUB, :] = dv[pl.ds(at, SUB), :].astype(BF16)
    heads = dq_0.shape[1] // HD
    for half in range(2):
        back[...] = (dq[half ^ meta[5]] * SCALE).T.astype(BF16)
        for step, out in enumerate((dq_0, dq_1, dq_2, dq_3)):
            for head in range(heads):
                at = pl.multiple_of(((meta[1] ^ step) * heads + head) * SPAN, SPAN)
                out[half * SPAN : (half + 1) * SPAN, head * HD : (head + 1) * HD] = back[pl.ds(at, SPAN), :]


def split_kernel(whole, grad_keys, grad_values, turned):
    _, sharer = place()
    wide = grad_keys.shape[0]
    for which, out in enumerate((grad_keys, grad_values)):
        pieces = []
        for half in range(2):
            at = (which * 2 + half) * SUB
            pieces += [whole[src, at : at + SUB, :] for src in range(4)]
        turned[...] = jnp.concatenate(pieces, axis=0).astype(F32).T
        out[...] = turned[pl.ds(pl.multiple_of(sharer * wide, wide), wide), :].astype(BF16)


def call(kernel, out_shape, scratch, flops, spaces, *args, limit=32, outs=None):
    return pl.pallas_call(
        kernel,
        out_shape=out_shape,
        in_specs=[pl.BlockSpec(memory_space={"s": pltpu.SMEM, "v": VM, "a": pl.ANY}[space]) for space in spaces],
        out_specs=outs or jax.tree.map(lambda _: pl.BlockSpec(memory_space=VM), out_shape),
        scratch_shapes=scratch,
        cost_estimate=pl.CostEstimate(flops=flops, bytes_accessed=1 << 20, transcendentals=0),
        compiler_params=pltpu.CompilerParams(vmem_limit_bytes=limit << 20),
    )(*args)


def on_device(queries, keys, values, grad_out, spans):
    rows, width = queries.shape
    ctx_count = lax.axis_size("ctx")
    spans = spans.T
    sds = jax.ShapeDtypeStruct
    blocks = sds((ctx_count, 4 * SUB, HD), BF16)
    kv_send = call(
        pick_kernel,
        blocks,
        [VM((4 * SUB, HD), BF16), pltpu.SemaphoreType.DMA((4,))],
        1 << 20,
        "aa",
        keys, values,
        limit=60,
    )
    kv = lax.all_to_all(kv_send, "ctx", 0, 0, tiled=True)
    qd, spans = call(
        pair_kernel,
        (sds((2, rows, width), BF16), sds(spans.shape, jnp.int32)),
        [],
        1 << 20,
        "vvv",
        queries, grad_out, spans,
    )
    crossed = lax.ppermute(qd, "pair", [(0, 1), (1, 0)])
    own = lax.all_gather(qd, "core", axis=0)
    other = lax.all_gather(crossed, "core", axis=0)
    stacked = 2 * 2 * (width // HD) * SPAN
    keys_held = 2 * ctx_count * SUB
    common = [VM((keys_held, HD), BF16)] * 2 + [VM((2, stacked, HD), BF16)] * 2
    mask = VM((TILE, WIDTH), jnp.int32)
    stats = call(
        stats_kernel,
        sds((8, stacked), F32),
        common + [VM((5, 8, stacked), F32), mask],
        1 << 30,
        "svvv",
        spans, kv, own, other,
    )
    stats_all = lax.all_gather(stats, ("pair", "core"), axis=0)
    dkv_send, dq_mine, *dq_send = call(
        grads_kernel,
        (blocks,) + (sds((rows, width), BF16),) * 4,
        common
        + [
            VM((2, 8, stacked), F32),
            VM((2, TILE, stacked), BF16),
            VM((2, TILE, stacked), BF16),
            VM((keys_held, HD), F32),
            VM((keys_held, HD), F32),
            VM((2, HD, stacked), F32),
            VM((HD, keys_held), BF16),
            VM((stacked, HD), BF16),
            mask,
        ],
        1 << 31,
        "svvvv",
        spans, stats_all, kv, own, other,
    )
    dkv = lax.all_to_all(dkv_send, "ctx", 0, 0, tiled=True)
    grad_queries = dq_mine.astype(F32)
    for step, piece in enumerate(dq_send, 1):
        grad_queries += lax.ppermute(piece, ("pair", "core"), [(i, i ^ step) for i in range(4)]).astype(F32)
    grad_queries = grad_queries.astype(BF16)
    summed = jnp.sum(dkv.astype(F32), axis=0).astype(BF16)
    whole = lax.all_gather(summed, ("pair", "core"), axis=0)
    part = sds((HD // 4, rows), BF16)
    grad_keys, grad_values = call(split_kernel, (part, part), [VM((HD, rows), F32)], 1 << 20, "v", whole)
    return (grad_queries, grad_keys.T, grad_values.T)


def solution(mesh):
    dp, ctx = mesh.devices.shape
    fine = Mesh(mesh.devices.reshape(dp // 4, 2, 2, ctx), ("group", "pair", "core", "ctx"))
    heads = ("group", "pair", "core")
    return jax.shard_map(
        on_device,
        mesh=fine,
        in_specs=(P("ctx", heads), P("ctx", None), P("ctx", None), P("ctx", heads), P()),
        out_specs=(P("ctx", heads), P("ctx", heads), P("ctx", heads)),
        check_vma=False,
    )
```

```python
import functools
import math

import jax
import jax.numpy as jnp
from jax import lax
from jax.experimental import pallas as pl
from jax.experimental.pallas import tpu as pltpu
from jax.sharding import Mesh
from jax.sharding import PartitionSpec as P

HD = 128
H = 64
KVH = 4
SPAN = 64
SUB = 16
TILE = 256
LOW = -1e30
FLOOR = -1e29
SCALE = 1.0 / math.sqrt(HD)
EXP2 = SCALE * math.log2(math.e)
VM = pltpu.VMEM
F32 = jnp.float32
BF16 = jnp.bfloat16
NT = (((1,), (1,)), ((), ()))
NN = (((1,), (0,)), ((), ()))


def dot(a, b, dims=NN):
    return lax.dot_general(a, b, dims, preferred_element_type=F32)


def place(spans=None):
    pair = lax.axis_index("pair")
    sharer = pair * 2 + lax.axis_index("core")
    if spans is None:
        return lax.axis_index("group"), sharer
    ctx = lax.axis_index("ctx")
    first, second = spans[0, ctx], spans[1, ctx]
    swapped = jnp.where(first > second, 1, 0)
    return lax.axis_index("group"), sharer, jnp.minimum(first, second), jnp.maximum(first, second), pair, swapped


def pick_kernel(keys, values, kv_out, held, sems):
    meta = place()
    col = pl.multiple_of(meta[0] * HD, HD)
    copies = []
    for which, ref in enumerate((keys, values)):
        for half in range(2):
            at = which * 2 + half
            row = pl.multiple_of(half * SPAN + meta[1] * SUB, SUB)
            copies.append(
                pltpu.make_async_copy(
                    ref.at[pl.ds(row, SUB), pl.ds(col, HD)], held.at[at * SUB : (at + 1) * SUB, :], sems.at[at]
                )
            )
    for copy in copies:
        copy.start()
    for copy in copies:
        copy.wait()
    for dest in range(kv_out.shape[0]):
        kv_out[dest] = held[...]


def pair_kernel(queries, cotan, spans, out, spans_out):
    spans_out[...] = spans[...]
    for which, ref in enumerate((queries, cotan)):
        for half in range(2):
            for head in range(ref.shape[1] // HD):
                rows = slice(half * SPAN, (half + 1) * SPAN)
                out[which, half, head * SPAN : (head + 1) * SPAN, :] = ref[rows, head * HD : (head + 1) * HD]


def piece(own, other, which, half, at):
    return (own, other)[at // 2][at % 2, which, half]


def to_local(meta, rows):
    middle = rows.shape[1] // 2
    turned = jnp.concatenate((rows[:, middle:], rows[:, :middle]), axis=1)
    return jnp.where(meta[4] == 1, turned, rows)


def sort_keys(spans, kv, ks, vs):
    for src in range(kv.shape[0]):
        for half in range(2):
            at = pl.multiple_of(spans[half, src] * SUB, SUB)
            ks[pl.ds(at, SUB), :] = kv[src, half * SUB : (half + 1) * SUB, :]
            vs[pl.ds(at, SUB), :] = kv[src, (2 + half) * SUB : (3 + half) * SUB, :]


def offsets():
    key = lax.broadcasted_iota(jnp.int32, (TILE, WIDTH), 0)
    row = lax.broadcasted_iota(jnp.int32, (TILE, WIDTH), 1)
    return (key >> 4) * SPAN + (key & (SUB - 1)) - (row & (SPAN - 1))


def units(meta):
    early = meta[2] < 16
    return (
        (0, 0, True),
        (1, 0, False),
        (1, 1, False),
        (1, 2, True),
        (jnp.where(early, 1, 0), jnp.where(early, 3, 1), True),
    )


def bound(meta, half, tile):
    span = jnp.where(half == 0, meta[2], meta[3])
    return span * SPAN - tile * (TILE // SUB * SPAN) - meta[1] * SUB


WIDTH = 256


def stats_kernel(spans, kv, own, other, out, ks, vs, part, off):
    meta = place(spans)
    off[...] = offsets()
    sort_keys(spans, kv, ks, vs)
    rows = out.shape[1]
    for unit, (half, tile, masked) in enumerate(units(meta)):
        at = pl.multiple_of(tile * TILE, TILE) if unit == 4 else tile * TILE
        key = ks[pl.ds(at, TILE), :]
        value = vs[pl.ds(at, TILE), :]
        for first in range(0, rows, WIDTH):
            cols = slice(first, first + WIDTH)
            score = dot(key, piece(own, other, 0, half ^ meta[5], first // WIDTH), NT)
            if masked:
                score = jnp.where(off[...] <= bound(meta, half, tile), score, LOW)
            top = jnp.maximum(jnp.max(score, axis=0, keepdims=True), FLOOR)
            weight = jnp.exp2((score - top) * EXP2)
            dprob = dot(value, piece(own, other, 1, half ^ meta[5], first // WIDTH), NT)
            part[unit, 0:1, cols] = top
            part[unit, 1:2, cols] = jnp.sum(weight, axis=0, keepdims=True)
            part[unit, 2:3, cols] = jnp.sum(weight * dprob, axis=0, keepdims=True)
    early = meta[2] < 16
    for half, mine in enumerate(((0,), (1, 2, 3))):
        extra = jnp.where(early, F32(half), F32(1 - half)) > 0.5
        tops = [part[unit, 0:1, :] for unit in mine] + [jnp.where(extra, part[4, 0:1, :], FLOOR)]
        top = functools.reduce(jnp.maximum, tops)
        total = jnp.zeros_like(top)
        weighted = jnp.zeros_like(top)
        for unit, unit_top in zip(mine + (4,), tops):
            factor = jnp.exp2((unit_top - top) * EXP2)
            if unit == 4:
                factor = jnp.where(extra, factor, 0.0)
            total = total + factor * part[unit, 1:2, :]
            weighted = weighted + factor * part[unit, 2:3, :]
        out[half * 3 : half * 3 + 1, :] = to_local(meta, top)
        out[half * 3 + 1 : half * 3 + 2, :] = to_local(meta, total)
        out[half * 3 + 2 : half * 3 + 3, :] = to_local(meta, weighted)
    out[6:8, :] = jnp.zeros((2, rows), F32)


def merge_stats(meta, stats, row_stats):
    for half in range(2):
        tops = [stats[src, half * 3 : half * 3 + 1, :] for src in range(4)]
        top = functools.reduce(jnp.maximum, tops)
        factors = [jnp.exp2((one - top) * EXP2) for one in tops]
        total = sum(factors[src] * stats[src, half * 3 + 1 : half * 3 + 2, :] for src in range(4))
        weighted = sum(factors[src] * stats[src, half * 3 + 2 : half * 3 + 3, :] for src in range(4))
        row_stats[half, 0:1, :] = to_local(meta, top)
        row_stats[half, 1:2, :] = to_local(meta, 1.0 / total)
        row_stats[half, 2:3, :] = to_local(meta, weighted / total)


def unit_grads(meta, ks, vs, own, other, row_stats, off, probs_b, dscore_b):
    rows = row_stats.shape[2]
    for unit, (half, tile, masked) in enumerate(units(meta)):
        at = pl.multiple_of(tile * TILE, TILE) if unit == 4 else tile * TILE
        key = ks[pl.ds(at, TILE), :]
        value = vs[pl.ds(at, TILE), :]
        for first in range(0, rows, WIDTH):
            cols = slice(first, first + WIDTH)
            score = dot(key, piece(own, other, 0, half ^ meta[5], first // WIDTH), NT)
            if masked:
                score = jnp.where(off[...] <= bound(meta, half, tile), score, LOW)
            prob = jnp.exp2((score - row_stats[half, 0:1, cols]) * EXP2) * row_stats[half, 1:2, cols]
            dprob = dot(value, piece(own, other, 1, half ^ meta[5], first // WIDTH), NT)
            dscore = prob * (dprob - row_stats[half, 2:3, cols])
            if probs_b is not None:
                probs_b[unit % 2, :, cols] = prob.astype(BF16)
            dscore_b[unit % 2, :, cols] = dscore.astype(BF16)
        yield unit, half, at


def key_grads_kernel(
    spans, stats, ks, vs, own, other, dkv_out, row_stats, probs_b, dscore_b, dk, dv, off
):
    meta = place(spans)
    off[...] = offsets()
    rows = row_stats.shape[2]
    merge_stats(meta, stats, row_stats)
    dk[3 * TILE :, :] = jnp.zeros((TILE, HD), F32)
    dv[3 * TILE :, :] = jnp.zeros((TILE, HD), F32)
    for unit, half, at in unit_grads(meta, ks, vs, own, other, row_stats, off, probs_b, dscore_b):
        keys_of = pl.ds(at, TILE)
        for which, ref, acc in ((1, probs_b, dv), (0, dscore_b, dk)):
            part = sum(
                dot(ref[unit % 2, :, first : first + WIDTH], piece(own, other, which, half ^ meta[5], first // WIDTH))
                for first in range(0, rows, WIDTH)
            )
            if unit in (0, 2, 3):
                acc[keys_of, :] = part
            else:
                acc[keys_of, :] += part
    for dest in range(dkv_out.shape[0]):
        for half in range(2):
            at = pl.multiple_of(spans[half, dest] * SUB, SUB)
            dkv_out[dest, half * SUB : (half + 1) * SUB, :] = (dk[pl.ds(at, SUB), :] * SCALE).astype(BF16)
            dkv_out[dest, (2 + half) * SUB : (3 + half) * SUB, :] = dv[pl.ds(at, SUB), :].astype(BF16)


def query_grads_kernel(
    spans, stats, ks, vs, own, other, dq_0, dq_1, dq_2, dq_3, row_stats, dscore_b, dq, kt, back, off
):
    meta = place(spans)
    off[...] = offsets()
    merge_stats(meta, stats, row_stats)
    kt[...] = ks[...].T
    for unit, half, at in unit_grads(meta, ks, vs, own, other, row_stats, off, None, dscore_b):
        dq_half = dot(kt[:, pl.ds(at, TILE)], dscore_b[unit % 2])
        if unit in (0, 1):
            dq[half] = dq_half
        else:
            dq[half] += dq_half
    heads = dq_0.shape[1] // HD
    for half in range(2):
        back[...] = (dq[half ^ meta[5]] * SCALE).T.astype(BF16)
        for step, out in enumerate((dq_0, dq_1, dq_2, dq_3)):
            for head in range(heads):
                sharer = step - step % 2 + ((meta[1] & 1) ^ (step % 2))
                at = pl.multiple_of((sharer * heads + head) * SPAN, SPAN)
                out[half * SPAN : (half + 1) * SPAN, head * HD : (head + 1) * HD] = back[pl.ds(at, SPAN), :]


def split_kernel(whole, grad_keys, grad_values, turned):
    _, sharer = place()
    wide = grad_keys.shape[0]
    for which, out in enumerate((grad_keys, grad_values)):
        pieces = []
        for half in range(2):
            at = (which * 2 + half) * SUB
            pieces += [whole[src, at : at + SUB, :] for src in range(4)]
        turned[...] = jnp.concatenate(pieces, axis=0).astype(F32).T
        out[...] = turned[pl.ds(pl.multiple_of(sharer * wide, wide), wide), :].astype(BF16)


def call(kernel, out_shape, scratch, flops, spaces, *args, limit=32, outs=None):
    return pl.pallas_call(
        kernel,
        out_shape=out_shape,
        in_specs=[pl.BlockSpec(memory_space={"s": pltpu.SMEM, "v": VM, "a": pl.ANY}[space]) for space in spaces],
        out_specs=outs or jax.tree.map(lambda _: pl.BlockSpec(memory_space=VM), out_shape),
        scratch_shapes=scratch,
        cost_estimate=pl.CostEstimate(flops=flops, bytes_accessed=1 << 20, transcendentals=0),
        compiler_params=pltpu.CompilerParams(vmem_limit_bytes=limit << 20),
    )(*args)


def on_device(queries, keys, values, grad_out, spans):
    rows, width = queries.shape
    ctx_count = lax.axis_size("ctx")
    spans = spans.T
    sds = jax.ShapeDtypeStruct
    blocks = sds((ctx_count, 4 * SUB, HD), BF16)
    kv_send = call(
        pick_kernel,
        blocks,
        [VM((4 * SUB, HD), BF16), pltpu.SemaphoreType.DMA((4,))],
        1 << 20,
        "aa",
        keys, values,
        limit=60,
    )
    kv = lax.all_to_all(kv_send, "ctx", 0, 0, tiled=True)
    heads = width // HD
    qd, spans = call(
        pair_kernel,
        (sds((2, 2, heads * SPAN, HD), BF16), sds(spans.shape, jnp.int32)),
        [],
        1 << 20,
        "vvv",
        queries, grad_out, spans,
    )
    crossed = lax.ppermute(qd, "pair", [(0, 1), (1, 0)])
    own = lax.all_gather(qd, "core", axis=0)
    other = lax.all_gather(crossed, "core", axis=0)
    stacked = 2 * 2 * heads * SPAN
    keys_held = 2 * ctx_count * SUB
    held = sds((keys_held, HD), BF16)
    mask = VM((TILE, WIDTH), jnp.int32)
    stats, ks, vs = call(
        stats_kernel,
        (sds((8, stacked), F32), held, held),
        [VM((5, 8, stacked), F32), mask],
        1 << 30,
        "svvv",
        spans, kv, own, other,
    )
    stats_all = lax.all_gather(stats, ("pair", "core"), axis=0)
    tiles = VM((2, TILE, stacked), BF16)
    row_stats = VM((2, 8, stacked), F32)
    dkv_send = call(
        key_grads_kernel,
        blocks,
        [row_stats, tiles, tiles, VM((keys_held, HD), F32), VM((keys_held, HD), F32), mask],
        1 << 31,
        "svvvvv",
        spans, stats_all, ks, vs, own, other,
    )
    dkv = lax.all_to_all(dkv_send, "ctx", 0, 0, tiled=True)
    dq_mine, *dq_send = call(
        query_grads_kernel,
        (sds((rows, width), BF16),) * 4,
        [
            row_stats,
            tiles,
            VM((2, HD, stacked), F32),
            VM((HD, keys_held), BF16),
            VM((stacked, HD), BF16),
            mask,
        ],
        1 << 31,
        "svvvvv",
        spans, stats_all, ks, vs, own, other,
    )
    grad_queries = dq_mine.astype(F32)
    for step, piece in enumerate(dq_send, 1):
        grad_queries += lax.ppermute(piece, ("pair", "core"), [(i, i ^ step) for i in range(4)]).astype(F32)
    grad_queries = grad_queries.astype(BF16)
    summed = jnp.sum(dkv.astype(F32), axis=0).astype(BF16)
    whole = lax.all_gather(summed, ("pair", "core"), axis=0)
    part = sds((HD // 4, rows), BF16)
    grad_keys, grad_values = call(split_kernel, (part, part), [VM((HD, rows), F32)], 1 << 20, "v", whole)
    return (grad_queries, grad_keys.T, grad_values.T)


def solution(mesh):
    dp, ctx = mesh.devices.shape
    fine = Mesh(mesh.devices.reshape(dp // 4, 2, 2, ctx), ("group", "pair", "core", "ctx"))
    heads = ("group", "pair", "core")
    return jax.shard_map(
        on_device,
        mesh=fine,
        in_specs=(P("ctx", heads), P("ctx", None), P("ctx", None), P("ctx", heads), P()),
        out_specs=(P("ctx", heads), P("ctx", heads), P("ctx", heads)),
        check_vma=False,
    )
```
